256 devices in a mesh: blk: 128 (over x, y_hi, z, core), grp: 2 (over y_lo).
Axes of the slice: x: 4, y: 4 (y_hi: 2, y_lo: 2; y = y_hi * 2 + y_lo), z: 8, core: 2. Of those that a mesh axis runs over, the one named last changes fastest.
Arguments:
- rows: float32 [2048, 1024], P(('blk', 'grp')), may hold values from -6 to 6
- lognorm: float32 [2048], P(('blk', 'grp')), may hold values from 3.5 to 5.5
- centroids: float32 [131072, 1024], P('blk'), may hold values from -0.1875 to 0.1875
- counts: int32 [131072], P('blk'), may hold values from 0 to 4096
Outputs:
- numerator: float32 [131072, 1024], P('blk')
- weights: float32 [131072], P('blk')
The draws below stay inside these ranges and needn't reach their ends.
All inputs are finite; a program needn't handle non-finite values.
Results may differ from the reference program's by a relative error of at most 0.0003.
Values sent between devices are 32-bit elements; how exact they have to be, the bound alone decides.
No kernel may reach another device: no remote copies, remote signals or barrier semaphores. Data moves between devices by JAX's collectives and lax.ppermute only.
A program may use at most 64 MiB of HBM per device.

```python
import jax
import jax.numpy as jnp
from jax import lax

D = 1024
CENTROIDS = 131072
ROWS = 2048


def plant(drawn, own_key, least, largest):
    longest = drawn.shape.index(max(drawn.shape))
    spots = []
    for shift in (0, 1):
        where = [jax.random.randint(jax.random.fold_in(own_key, axis), (), 0, length) for axis, length in enumerate(drawn.shape)]
        where[longest] = (where[longest] + shift) % drawn.shape[longest]
        spots.append(tuple(where))
    return drawn.at[spots[0]].set(least).at[spots[1]].set(largest)


def block_scale(rng, dims, cuts, low, top_value):
    gain = 1.0
    for axis_at, parts in cuts:
        draws = jax.random.uniform(jax.random.fold_in(jax.random.fold_in(rng, 6), axis_at), (parts,), jnp.float32, low / len(cuts), top_value / len(cuts))
        gain = gain * jnp.repeat(jnp.exp(draws), dims[axis_at] // parts).reshape((-1,) + (1,) * (len(dims) - 1 - axis_at))
    return gain


def noise(stream_key, extent, deviation, limit, shards=(), kind=jnp.bfloat16):
    entries = jax.random.normal(stream_key, extent, jnp.float32) * deviation
    if len(shards) > 0:
        entries = block_scale(stream_key, extent, shards, -0.22, 0.18) * entries
    return jnp.clip(entries, min=-limit, max=limit).astype(kind)


def setup_inputs(seed: int = 0) -> dict:
    key_list = jax.random.split(jax.random.key(seed), 5)
    return {
        "rows": noise(key_list[0], (ROWS, D), 1.0, 6.0, ((0, 256),), jnp.float32),
        "lognorm": jnp.clip(3.5 + 2.0 * jax.random.uniform(key_list[1], (ROWS,), jnp.float32) ** block_scale(key_list[1], (ROWS,), ((0, 256),), -0.2, 0.2), 3.5, 5.5),
        "centroids": noise(key_list[2], (CENTROIDS, D), D ** -0.5, 0.1875, ((0, 128),), jnp.float32),
        "counts": plant(jax.random.randint(key_list[3], (CENTROIDS,), 0, 4097), jax.random.fold_in(key_list[3], 1), 0, 4096).astype(jnp.int32),
    }


def reference(rows, lognorm, centroids, counts):
    penalty = 0.5 * jnp.log1p(counts.astype(jnp.float32))
    block = min(256, ROWS)
    row_blocks = rows.reshape(ROWS // block, block, D)
    norm_blocks = lognorm.reshape(ROWS // block, block)

    def step(carry, items):
        part_rows, part_norm = items
        score = jnp.dot(part_rows, centroids.T, precision=lax.Precision.HIGHEST, preferred_element_type=jnp.float32)
        resp = jnp.exp(score - penalty[None, :] - part_norm[:, None])
        total = carry[0] + jnp.dot(resp.T, part_rows, precision=lax.Precision.HIGHEST, preferred_element_type=jnp.float32)
        mass = carry[1] + jnp.sum(resp, axis=0)
        return (total, mass), None

    start = (jnp.zeros((CENTROIDS, D), jnp.float32), jnp.zeros((CENTROIDS,), jnp.float32))
    (numerator, weights), _ = lax.scan(step, start, (row_blocks, norm_blocks))
    return numerator, weights
```

```python
import functools

import jax
import jax.numpy as jnp
from jax import lax
from jax.experimental import pallas as pl
from jax.experimental.pallas import tpu as pltpu
from jax.sharding import Mesh, PartitionSpec as P

f32, bf16 = jnp.float32, jnp.bfloat16
AXES = ("x", "yh", "z", "core", "yl")
NT = (((1,), (1,)), ((), ()))
NN = (((1,), (0,)), ((), ()))
LANES = 128
VMEM = pl.BlockSpec(memory_space=pltpu.VMEM)


def flat(x, y, z, c):
    return ((x % 4 * 2 + y % 4 // 2) * 8 + z % 8) * 4 + c * 2 + y % 2


def pairs(target):
    return [
        (flat(x, y, z, c), flat(*target(x, y, z, c)))
        for x in range(4) for y in range(4) for z in range(8) for c in range(2)
    ]


LOOP = [(0, 0), (1, 0), (2, 0), (3, 0), (3, 1), (2, 1), (1, 1), (0, 1)]


def ring(step):
    def target(x, y, z, c):
        if c == 0:
            return x, y, z + step, c
        nx, ny = LOOP[(LOOP.index((x, y % 2)) + step) % 8]
        return nx, y // 2 * 2 + ny, z, c
    return pairs(target)


FORWARD, BACKWARD = ring(1), ring(-1)
SWAP = pairs(lambda x, y, z, c: (x, y, z, 1 - c))
FIRST = [[flat(x, y, z, 0) for x in range(4) for y in range(4)] for z in range(8)] + [
    [flat(x, 2 * yh + yl, z, 1) for z in range(8) for yh in range(2)] for x in range(4) for yl in range(2)
]


def halves(v):
    high = v.astype(bf16)
    return high, (v - high.astype(f32)).astype(bf16)


def dot(a, b, dims):
    return lax.dot_general(a, b, dims, preferred_element_type=f32)


def product(a_high, a_low, b_high, b_low, dims):
    return dot(a_high, b_high, dims) + dot(a_low, b_high, dims) + dot(a_high, b_low, dims)


def prepare_kernel(shard, counts, high, low, penalty):
    high[...], low[...] = halves(shard[...])
    pen = 0.5 * jnp.log(1.0 + counts[...].astype(f32))
    for i in range(8):
        penalty[pl.ds(i * LANES, LANES), :] = jnp.transpose(jnp.broadcast_to(pen[i : i + 1, :], (LANES, LANES)))


def prepare(shard, counts):
    k, d = shard.shape
    return pl.pallas_call(
        prepare_kernel,
        in_specs=[VMEM] * 2,
        out_specs=[VMEM] * 3,
        out_shape=[pltpu.VMEM((k, d), bf16), pltpu.VMEM((k, d), bf16), pltpu.VMEM((k, LANES), f32)],
        compiler_params=pltpu.CompilerParams(vmem_limit_bytes=8 * 2**20),
        cost_estimate=pl.CostEstimate(flops=4 * k * d, bytes_accessed=8 * k * d, transcendentals=0),
        name="prepare",
    )(in_vmem(shard), in_vmem(counts.reshape(8, LANES)))


def in_vmem(v):
    return pltpu.with_memory_space_constraint(v, pltpu.VMEM)


def load_rows(blocks, row_high, row_low):
    norms = []
    d = row_high.shape[1]
    for i, block in enumerate(blocks):
        n = block.shape[0]
        row_high[pl.ds(i * n, n), :], row_low[pl.ds(i * n, n), :] = halves(block[:, :d])
        norms.append(jnp.transpose(block[:, d:])[0:1, :])
    return jnp.concatenate(norms, axis=1)


def responses(high, low, penalty, norms, row_high, row_low, at):
    score = product(high[at, :], low[at, :], row_high[...], row_low[...], NT)
    resp = jnp.exp(score - penalty[at, 0:1] - norms)
    total = product(*halves(resp), row_high[...], row_low[...], NN)
    mass = sum(resp[:, i : i + LANES] for i in range(0, resp.shape[1], LANES))
    return total, mass


def chunk_kernel(count, fresh, step, *refs):
    blocks, refs = refs[:count], refs[count:]
    if fresh:
        high, low, penalty, total_out, mass_out, row_high, row_low = refs
    else:
        high, low, penalty, total_in, mass_in, total_out, mass_out, row_high, row_low = refs
    norms = load_rows(blocks, row_high, row_low)
    for start in range(0, high.shape[0], step):
        at = pl.ds(start, step)
        total, mass = responses(high, low, penalty, norms, row_high, row_low, at)
        if fresh:
            total_out[at, :], mass_out[at, :] = total, mass
        else:
            total_out[at, :], mass_out[at, :] = total_in[at, :] + total, mass_in[at, :] + mass


def cost(rows, k, d):
    return pl.CostEstimate(flops=12 * rows * k * d, bytes_accessed=4 * rows * d, transcendentals=rows * k)


def chunk(blocks, high, low, penalty, sums):
    k, d = high.shape
    count, rows = len(blocks), sum(b.shape[0] for b in blocks)
    args = [*blocks, high, low, penalty, *sums]
    return pl.pallas_call(
        functools.partial(chunk_kernel, count, not sums, 512),
        in_specs=[VMEM] * len(args),
        out_specs=[VMEM] * 2,
        out_shape=[pltpu.VMEM((k, d), f32), pltpu.VMEM((k, LANES), f32)],
        scratch_shapes=[pltpu.VMEM((rows, d), bf16)] * 2,
        input_output_aliases={count + 3: 0, count + 4: 1} if sums else {},
        compiler_params=pltpu.CompilerParams(vmem_limit_bytes=20 * 2**20),
        cost_estimate=cost(rows, k, d),
        name="chunk",
    )(*[in_vmem(a) for a in args])


def last_kernel(count, step, *refs):
    blocks, refs = refs[:count], refs[count:]
    high, low, penalty, total_in, mass_in, total_out, mass_out, row_high, row_low, norm_row = refs
    i = pl.program_id(0)

    @pl.when(i == 0)
    def _():
        norm_row[0:1, :] = load_rows(blocks, row_high, row_low)

    at = pl.ds(pl.multiple_of(i * step, step), step)
    total, mass = responses(high, low, penalty, norm_row[0:1, :], row_high, row_low, at)
    total_out[...] = total_in[at, :] + total
    mass = mass_in[at, :] + mass
    for j in range(step // LANES):
        part = jnp.transpose(mass[j * LANES : (j + 1) * LANES, :])
        mass_out[0, j : j + 1, :] = jnp.sum(part, axis=0, keepdims=True)


def last(blocks, high, low, penalty, sums):
    k, d = high.shape
    step = 256
    count, rows = len(blocks), sum(b.shape[0] for b in blocks)
    args = [*blocks, high, low, penalty, *sums]
    numerator, weights = pl.pallas_call(
        functools.partial(last_kernel, count, step),
        grid=(k // step,),
        in_specs=[VMEM] * len(args),
        out_specs=[
            pl.BlockSpec((step, d), lambda i: (i, 0)),
            pl.BlockSpec((1, step // LANES, LANES), lambda i: (i, 0, 0)),
        ],
        out_shape=[jax.ShapeDtypeStruct((k, d), f32), jax.ShapeDtypeStruct((k // step, step // LANES, LANES), f32)],
        scratch_shapes=[pltpu.VMEM((rows, d), bf16)] * 2 + [pltpu.VMEM((8, rows), f32)],
        compiler_params=pltpu.CompilerParams(vmem_limit_bytes=20 * 2**20),
        cost_estimate=cost(rows, k, d),
        name="last",
    )(*[in_vmem(a) for a in args])
    return numerator, weights.reshape(k)


def body(rows, lognorm, centroids, counts):
    def send(v, how):
        return lax.ppermute(v, AXES, how)

    n = rows.shape[0]
    own = jnp.concatenate([rows, jnp.broadcast_to(lognorm[:, None], (n, LANES))], axis=1)
    own = lax.all_to_all(
        jnp.broadcast_to(own, (16, *own.shape)), AXES, 0, 0, axis_index_groups=FIRST, tiled=True
    ).reshape(16 * n, -1)
    prepared = prepare(centroids, counts)
    up, down = send(own, FORWARD), send(own, BACKWARD)
    sums = chunk([own, send(own, SWAP)], *prepared, ())
    for _ in range(2):
        blocks = [up, down]
        up, down = send(up, FORWARD), send(down, BACKWARD)
        sums = chunk(blocks + [send(b, SWAP) for b in blocks], *prepared, sums)
    blocks = [up, down]
    up = send(up, FORWARD)
    sums = chunk(blocks + [send(b, SWAP) for b in blocks], *prepared, sums)
    return last([up, send(up, SWAP)], *prepared, sums)


def solution(mesh):
    split = Mesh(mesh.devices.reshape(4, 2, 8, 2, 2), AXES)
    blk = ("x", "yh", "z", "core")
    in_specs = (P(AXES, None), P(AXES), P(blk, None), P(blk))
    out_specs = (P(blk, None), P(blk))
    return jax.shard_map(body, mesh=split, in_specs=in_specs, out_specs=out_specs, check_vma=False)
```

```python
import functools

import jax
import jax.numpy as jnp
from jax import lax
from jax.experimental import pallas as pl
from jax.experimental.pallas import tpu as pltpu
from jax.sharding import Mesh, PartitionSpec as P

f32, bf16 = jnp.float32, jnp.bfloat16
AXES = ("x", "yh", "z", "core", "yl")
NT = (((1,), (1,)), ((), ()))
NN = (((1,), (0,)), ((), ()))
LANES = 128
VMEM = pl.BlockSpec(memory_space=pltpu.VMEM)


def flat(x, y, z, c):
    return ((x % 4 * 2 + y % 4 // 2) * 8 + z % 8) * 4 + c * 2 + y % 2


def pairs(target):
    return [
        (flat(x, y, z, c), flat(*target(x, y, z, c)))
        for x in range(4) for y in range(4) for z in range(8) for c in range(2)
    ]


LOOP = [(0, 0), (1, 0), (2, 0), (3, 0), (3, 1), (2, 1), (1, 1), (0, 1)]


def ring(step):
    def target(x, y, z, c):
        if c == 0:
            return x, y, z + step, c
        yh, yl = y // 2, y % 2
        nx, nh = LOOP[(LOOP.index(((x + 2 * yl) % 4, yh)) + step) % 8]
        return nx + 2 * yl, nh * 2 + yl, z, c
    return pairs(target)


FORWARD, BACKWARD = ring(1), ring(-1)
SWAP = pairs(lambda x, y, z, c: (x, y, z, 1 - c))
FIRST = [[flat(x, y, z, 0) for x in range(4) for y in range(4)] for z in range(8)] + [
    [flat(x, 2 * yh + yl, z, 1) for z in range(8) for yl in range(2)] for x in range(4) for yh in range(2)
]


def halves(v):
    high = v.astype(bf16)
    return high, (v - high.astype(f32)).astype(bf16)


def dot(a, b, dims):
    return lax.dot_general(a, b, dims, preferred_element_type=f32)


def product(a_high, a_low, b_high, b_low, dims):
    return dot(a_high, b_high, dims) + dot(a_low, b_high, dims) + dot(a_high, b_low, dims)


def prepare_kernel(parts, shard, counts, high, low, penalty, landed, sems):
    n = shard.shape[0] // parts
    places = [pl.ds(i * n, n) for i in range(parts)]
    copies = [pltpu.make_async_copy(shard.at[at, :], landed.at[at, :], sems.at[i]) for i, at in enumerate(places)]
    for copy in copies:
        copy.start()
    pen = 0.5 * jnp.log(1.0 + counts[...].astype(f32))
    for i in range(pen.shape[0]):
        penalty[pl.ds(i * LANES, LANES), :] = jnp.transpose(jnp.broadcast_to(pen[i : i + 1, :], (LANES, LANES)))
    for copy, at in zip(copies, places):
        copy.wait()
        high[at, :], low[at, :] = halves(landed[at, :])


def prepare(shard, counts):
    k, d = shard.shape
    parts = 8
    return pl.pallas_call(
        functools.partial(prepare_kernel, parts),
        in_specs=[pl.BlockSpec(memory_space=pl.ANY), VMEM],
        out_specs=[VMEM] * 3,
        out_shape=[pltpu.VMEM((k, d), bf16), pltpu.VMEM((k, d), bf16), pltpu.VMEM((k, LANES), f32)],
        scratch_shapes=[pltpu.VMEM((k, d), f32), pltpu.SemaphoreType.DMA((parts,))],
        compiler_params=pltpu.CompilerParams(vmem_limit_bytes=8 * 2**20),
        cost_estimate=pl.CostEstimate(flops=4 * k * d, bytes_accessed=8 * k * d, transcendentals=0),
        name="prepare",
    )(pltpu.with_memory_space_constraint(shard, pltpu.HBM), counts.reshape(k // LANES, LANES))


def pack_kernel(rows, norms, packed):
    n, d = rows.shape
    diagonal = lax.broadcasted_iota(jnp.int32, (n, n), 0) == lax.broadcasted_iota(jnp.int32, (n, n), 1)
    norm = jnp.sum(jnp.where(diagonal, norms[...], 0.0), axis=1, keepdims=True)
    packed[:, :, :d] = jnp.broadcast_to(rows[...][None], (packed.shape[0], n, d))
    packed[:, :, d:] = jnp.broadcast_to(norm[None], (packed.shape[0], n, LANES))


def pack(rows, lognorm, copies):
    n, d = rows.shape
    return pl.pallas_call(
        pack_kernel,
        in_specs=[VMEM] * 2,
        out_specs=VMEM,
        out_shape=pltpu.VMEM((copies, n, d + LANES), f32),
        name="pack",
    )(rows, lognorm.reshape(1, n))


MARGIN = 8


def join_kernel(parts, joined):
    count, n, width = parts.shape
    half, d = count // 2 * n, joined.shape[1]
    for i in range(count):
        joined[pl.ds(i * n + (i >= count // 2) * MARGIN, n), :] = parts[i, :, :d]
    norms = jnp.transpose(parts[:, :, d:].reshape(count * n, LANES))[:MARGIN, :]
    joined[pl.ds(half, MARGIN), :] = jnp.concatenate([norms, jnp.zeros((MARGIN, d - count * n), f32)], axis=1)


def join(parts):
    count, n, width = parts.shape
    return pl.pallas_call(
        join_kernel,
        in_specs=[VMEM],
        out_specs=VMEM,
        out_shape=pltpu.VMEM((count * n + MARGIN, width - LANES), f32),
        name="join",
    )(in_vmem(parts))


def in_vmem(v):
    return pltpu.with_memory_space_constraint(v, pltpu.VMEM)


def load_rows(blocks, row_high, row_low):
    norms, row = [], 0
    for kind, block in blocks:
        n = block.shape[0] - MARGIN
        middle = {"whole": n // 2, "front": n, "back": 0}[kind]
        first = n if kind == "back" else 0
        norms.append(block[middle : middle + 1, first : first + n])
        for start, end in ((0, middle), (middle + MARGIN, n + MARGIN)):
            if start < end:
                at = pl.ds(row, end - start)
                row_high[at, :], row_low[at, :] = halves(block[start:end, :])
                row += end - start
    return jnp.concatenate(norms, axis=1)


def rows_in(blocks):
    return sum(b.shape[0] - MARGIN for b in blocks)


def respond(high, low, penalty, norms, row_high, row_low, resp_high, resp_low, at):
    score = product(high[at, :], low[at, :], row_high[...], row_low[...], NT)
    resp = jnp.exp(score - penalty[at, 0:1] - norms)
    resp_high[at, :], resp_low[at, :] = halves(resp)
    return sum(resp[:, i : i + LANES] for i in range(0, resp.shape[1], LANES))


def gather_up(row_high, row_low, resp_high, resp_low, at):
    return product(resp_high[at, :], resp_low[at, :], row_high[...], row_low[...], NN)


def chunk_kernel(kinds, fresh, step, *refs):
    count = len(kinds)
    blocks, refs = list(zip(kinds, refs[:count])), refs[count:]
    if fresh:
        high, low, penalty, total_out, mass_out, *work = refs
    else:
        high, low, penalty, total_in, mass_in, total_out, mass_out, *work = refs
    norms = load_rows(blocks, *work[:2])
    places = [pl.ds(start, step) for start in range(0, high.shape[0], step)]
    for at in places:
        mass = respond(high, low, penalty, norms, *work, at)
        mass_out[at, :] = mass if fresh else mass_in[at, :] + mass
    for at in places:
        total = gather_up(*work, at)
        total_out[at, :] = total if fresh else total_in[at, :] + total


def scratch(rows, k, d):
    return [pltpu.VMEM((rows, d), bf16)] * 2 + [pltpu.VMEM((k, rows), bf16)] * 2


def cost(rows, k, d):
    return pl.CostEstimate(flops=12 * rows * k * d, bytes_accessed=4 * rows * d, transcendentals=rows * k)


def chunk(blocks, high, low, penalty, sums):
    k, d = high.shape
    count, rows = len(blocks), rows_in(blocks)
    args = [*blocks, high, low, penalty, *sums]
    return pl.pallas_call(
        functools.partial(chunk_kernel, ["whole"] * count, not sums, 512),
        in_specs=[VMEM] * len(args),
        out_specs=[VMEM] * 2,
        out_shape=[pltpu.VMEM((k, d), f32), pltpu.VMEM((k, LANES), f32)],
        scratch_shapes=scratch(rows, k, d),
        input_output_aliases={count + 3: 0, count + 4: 1} if sums else {},
        compiler_params=pltpu.CompilerParams(vmem_limit_bytes=20 * 2**20),
        cost_estimate=cost(rows, k, d),
        name="chunk",
    )(*[in_vmem(a) for a in args])


def last_kernel(kinds, step, out_step, *refs):
    count = len(kinds)
    blocks, refs = list(zip(kinds, refs[:count])), refs[count:]
    high, low, penalty, total_in, mass_in, total_out, mass_out, done, sems, *work = refs
    norms = load_rows(blocks, *work[:2])
    k = high.shape[0]
    for start in range(0, k, step):
        at = pl.ds(start, step)
        mass = mass_in[at, :] + respond(high, low, penalty, norms, *work, at)
        for j in range(step // LANES):
            part = jnp.transpose(mass[j * LANES : (j + 1) * LANES, :])
            mass_out[pl.ds(start // LANES + j, 1), :] = jnp.sum(part, axis=0, keepdims=True)
    copies = []
    for i, start in enumerate(range(0, k, out_step)):
        at = pl.ds(start, out_step)
        done[at, :] = total_in[at, :] + gather_up(*work, at)
        copies.append(pltpu.make_async_copy(done.at[at, :], total_out.at[at, :], sems.at[i]))
        copies[-1].start()
    for copy in copies:
        copy.wait()


def last(blocks, high, low, penalty, sums):
    k, d = high.shape
    step, out_step = 512, 128
    count, rows = len(blocks), rows_in(blocks)
    args = [*blocks, high, low, penalty, *sums]
    numerator, weights = pl.pallas_call(
        functools.partial(last_kernel, ["front", "back"] * (count // 2), step, out_step),
        in_specs=[VMEM] * len(args),
        out_specs=[pl.BlockSpec(memory_space=pl.ANY), VMEM],
        out_shape=[jax.ShapeDtypeStruct((k, d), f32), jax.ShapeDtypeStruct((k // LANES, LANES), f32)],
        scratch_shapes=[pltpu.VMEM((k, d), f32), pltpu.SemaphoreType.DMA((k // out_step,))] + scratch(rows, k, d),
        compiler_params=pltpu.CompilerParams(vmem_limit_bytes=20 * 2**20),
        cost_estimate=cost(rows, k, d),
        name="last",
    )(*[in_vmem(a) for a in args])
    return numerator, weights.reshape(k)


def after(v, other):
    return lax.optimization_barrier((v, other))[0]


def body(rows, lognorm, centroids, counts):
    def send(v, how):
        return lax.ppermute(v, AXES, how)

    own = lax.all_to_all(pack(rows, lognorm, 16), AXES, 0, 0, axis_index_groups=FIRST, tiled=True)
    own = join(own)
    prepared = prepare(centroids, counts)
    up, down = send(own, FORWARD), send(own, BACKWARD)
    sums = chunk([own, send(own, SWAP)], *prepared, ())
    for _ in range(2):
        up, down, sums = after(up, sums), after(down, sums), after(sums, (up, down))
        blocks = [after(up, down), after(down, up)]
        up, down = send(up, FORWARD), send(down, BACKWARD)
        sums = chunk(blocks + [send(b, SWAP) for b in blocks], *prepared, sums)
    up, down, sums = after(up, sums), after(down, sums), after(sums, (up, down))
    half = rows_in([up]) // 2
    far = [send(up[: half + MARGIN], FORWARD), send(down[half:], BACKWARD)]
    up, down = after(up, down), after(down, up)
    swapped = [send(up, SWAP), send(down, SWAP)]
    sums = chunk([up, down], *prepared, sums)
    far, sums = after(far, sums), after(sums, far)
    far_swapped = [send(b, SWAP) for b in far]
    sums = chunk(swapped, *prepared, sums)
    return last(far + far_swapped, *prepared, sums)


def solution(mesh):
    split = Mesh(mesh.devices.reshape(4, 2, 8, 2, 2), AXES)
    blk = ("x", "yh", "z", "core")
    in_specs = (P(AXES, None), P(AXES), P(blk, None), P(blk))
    out_specs = (P(blk, None), P(blk))
    return jax.shard_map(body, mesh=split, in_specs=in_specs, out_specs=out_specs, check_vma=False)
```

```python
import functools

import jax
import jax.numpy as jnp
from jax import lax
from jax.experimental import pallas as pl
from jax.experimental.pallas import tpu as pltpu
from jax.sharding import Mesh, PartitionSpec as P

f32, bf16 = jnp.float32, jnp.bfloat16
AXES = ("x", "yh", "z", "core", "yl")
NT = (((1,), (1,)), ((), ()))
NN = (((1,), (0,)), ((), ()))
LANES = 128
VMEM = pl.BlockSpec(memory_space=pltpu.VMEM)


def flat(x, y, z, c):
    return ((x % 4 * 2 + y % 4 // 2) * 8 + z % 8) * 4 + c * 2 + y % 2


def pairs(target):
    return [
        (flat(x, y, z, c), flat(*target(x, y, z, c)))
        for x in range(4) for y in range(4) for z in range(8) for c in range(2)
    ]


LOOP = [(0, 0), (1, 0), (2, 0), (3, 0), (3, 1), (2, 1), (1, 1), (0, 1)]


def ring(step):
    def target(x, y, z, c):
        if c == 0:
            return x, y, z + step, c
        yh, yl = y // 2, y % 2
        nx, nh = LOOP[(LOOP.index(((x + 2 * yl) % 4, yh)) + step) % 8]
        return nx + 2 * yl, nh * 2 + yl, z, c
    return pairs(target)


FORWARD, BACKWARD = ring(1), ring(-1)
SWAP = pairs(lambda x, y, z, c: (x, y, z, 1 - c))
FIRST = [[flat(x, y, z, 0) for x in range(4) for y in range(4)] for z in range(8)] + [
    [flat(x, 2 * yh + yl, z, 1) for z in range(8) for yl in range(2)] for x in range(4) for yh in range(2)
]


def halves(v):
    high = v.astype(bf16)
    return high, (v - high.astype(f32)).astype(bf16)


def dot(a, b, dims):
    return lax.dot_general(a, b, dims, preferred_element_type=f32)


def product(a_high, a_low, b_high, b_low, dims):
    return dot(a_high, b_high, dims) + dot(a_low, b_high, dims) + dot(a_high, b_low, dims)


def prepare_kernel(parts, shard, counts, high, low, penalty, landed, sems):
    n = shard.shape[0] // parts
    places = [pl.ds(i * n, n) for i in range(parts)]
    copies = [pltpu.make_async_copy(shard.at[at, :], landed.at[at, :], sems.at[i]) for i, at in enumerate(places)]
    for copy in copies:
        copy.start()
    pen = 0.5 * jnp.log(1.0 + counts[...].astype(f32))
    for i in range(pen.shape[0]):
        penalty[pl.ds(i * LANES, LANES), :] = jnp.transpose(jnp.broadcast_to(pen[i : i + 1, :], (LANES, LANES)))
    for copy, at in zip(copies, places):
        copy.wait()
        high[at, :], low[at, :] = halves(landed[at, :])


def prepare(shard, counts):
    k, d = shard.shape
    parts = 8
    return pl.pallas_call(
        functools.partial(prepare_kernel, parts),
        in_specs=[pl.BlockSpec(memory_space=pl.ANY), VMEM],
        out_specs=[VMEM] * 3,
        out_shape=[pltpu.VMEM((k, d), bf16), pltpu.VMEM((k, d), bf16), pltpu.VMEM((k, LANES), f32)],
        scratch_shapes=[pltpu.VMEM((k, d), f32), pltpu.SemaphoreType.DMA((parts,))],
        compiler_params=pltpu.CompilerParams(vmem_limit_bytes=8 * 2**20),
        cost_estimate=pl.CostEstimate(flops=4 * k * d, bytes_accessed=8 * k * d, transcendentals=0),
        name="prepare",
    )(pltpu.with_memory_space_constraint(shard, pltpu.HBM), counts.reshape(k // LANES, LANES))


def pack_kernel(rows, norms, packed):
    n, d = rows.shape
    diagonal = lax.broadcasted_iota(jnp.int32, (n, n), 0) == lax.broadcasted_iota(jnp.int32, (n, n), 1)
    norm = jnp.sum(jnp.where(diagonal, norms[...], 0.0), axis=1, keepdims=True)
    packed[:, :, :d] = jnp.broadcast_to(rows[...][None], (packed.shape[0], n, d))
    packed[:, :, d:] = jnp.broadcast_to(norm[None], (packed.shape[0], n, LANES))


def pack(rows, lognorm, copies):
    n, d = rows.shape
    return pl.pallas_call(
        pack_kernel,
        in_specs=[VMEM] * 2,
        out_specs=VMEM,
        out_shape=pltpu.VMEM((copies, n, d + LANES), f32),
        name="pack",
    )(rows, lognorm.reshape(1, n))


MARGIN = 8


def join_kernel(parts, joined):
    count, n, width = parts.shape
    rows, d = count * n, joined.shape[1]
    joined[pl.ds(0, rows), :] = parts[:, :, :d].reshape(rows, d)
    norms = jnp.transpose(parts[:, :, d:].reshape(rows, LANES))[:MARGIN, :]
    joined[pl.ds(rows, MARGIN), :] = jnp.concatenate([norms, jnp.zeros((MARGIN, d - rows), f32)], axis=1)


def join(parts):
    count, n, width = parts.shape
    return pl.pallas_call(
        join_kernel,
        in_specs=[VMEM],
        out_specs=VMEM,
        out_shape=pltpu.VMEM((count * n + MARGIN, width - LANES), f32),
        name="join",
    )(in_vmem(parts))


def in_vmem(v):
    return pltpu.with_memory_space_constraint(v, pltpu.VMEM)


def load_rows(blocks, row_high, row_low):
    norms = []
    for i, block in enumerate(blocks):
        n = block.shape[0] - MARGIN
        at = pl.ds(i * n, n)
        row_high[at, :], row_low[at, :] = halves(block[:n, :])
        norms.append(block[n : n + 1, :n])
    return jnp.concatenate(norms, axis=1)


def rows_in(blocks):
    return sum(b.shape[0] - MARGIN for b in blocks)


def respond(high, low, penalty, norms, row_high, row_low, resp_high, resp_low, at):
    score = product(high[at, :], low[at, :], row_high[...], row_low[...], NT)
    resp = jnp.exp(score - penalty[at, 0:1] - norms)
    resp_high[at, :], resp_low[at, :] = halves(resp)
    return sum(resp[:, i : i + LANES] for i in range(0, resp.shape[1], LANES))


def gather_up(row_high, row_low, resp_high, resp_low, at):
    return product(resp_high[at, :], resp_low[at, :], row_high[...], row_low[...], NN)


def chunk_kernel(count, fresh, step, *refs):
    blocks, refs = refs[:count], refs[count:]
    if fresh:
        high, low, penalty, total_out, mass_out, *work = refs
    else:
        high, low, penalty, total_in, mass_in, total_out, mass_out, *work = refs
    norms = load_rows(blocks, *work[:2])
    places = [pl.ds(start, step) for start in range(0, high.shape[0], step)]
    for at in places:
        mass = respond(high, low, penalty, norms, *work, at)
        mass_out[at, :] = mass if fresh else mass_in[at, :] + mass
    for at in places:
        total = gather_up(*work, at)
        total_out[at, :] = total if fresh else total_in[at, :] + total


def scratch(rows, k, d):
    return [pltpu.VMEM((rows, d), bf16)] * 2 + [pltpu.VMEM((k, rows), bf16)] * 2


def cost(rows, k, d):
    return pl.CostEstimate(flops=12 * rows * k * d, bytes_accessed=4 * rows * d, transcendentals=rows * k)


def chunk(blocks, high, low, penalty, sums):
    k, d = high.shape
    count, rows = len(blocks), rows_in(blocks)
    args = [*blocks, high, low, penalty, *sums]
    return pl.pallas_call(
        functools.partial(chunk_kernel, count, not sums, 512),
        in_specs=[VMEM] * len(args),
        out_specs=[VMEM] * 2,
        out_shape=[pltpu.VMEM((k, d), f32), pltpu.VMEM((k, LANES), f32)],
        scratch_shapes=scratch(rows, k, d),
        input_output_aliases={count + 3: 0, count + 4: 1} if sums else {},
        compiler_params=pltpu.CompilerParams(vmem_limit_bytes=20 * 2**20),
        cost_estimate=cost(rows, k, d),
        name="chunk",
    )(*[in_vmem(a) for a in args])


def last_kernel(count, step, out_step, *refs):
    blocks, refs = refs[:count], refs[count:]
    high, low, penalty, total_in, mass_in, total_out, mass_out, done, sems, *work = refs
    norms = load_rows(blocks, *work[:2])
    k = high.shape[0]
    for start in range(0, k, step):
        at = pl.ds(start, step)
        mass = mass_in[at, :] + respond(high, low, penalty, norms, *work, at)
        for j in range(step // LANES):
            part = jnp.transpose(mass[j * LANES : (j + 1) * LANES, :])
            mass_out[pl.ds(start // LANES + j, 1), :] = jnp.sum(part, axis=0, keepdims=True)
    copies = []
    for i, start in enumerate(range(0, k, out_step)):
        at = pl.ds(start, out_step)
        done[at, :] = total_in[at, :] + gather_up(*work, at)
        copies.append(pltpu.make_async_copy(done.at[at, :], total_out.at[at, :], sems.at[i]))
        copies[-1].start()
    for copy in copies:
        copy.wait()


def last(blocks, high, low, penalty, sums):
    k, d = high.shape
    step, out_step = 512, 128
    count, rows = len(blocks), rows_in(blocks)
    args = [*blocks, high, low, penalty, *sums]
    numerator, weights = pl.pallas_call(
        functools.partial(last_kernel, count, step, out_step),
        in_specs=[VMEM] * len(args),
        out_specs=[pl.BlockSpec(memory_space=pl.ANY), VMEM],
        out_shape=[jax.ShapeDtypeStruct((k, d), f32), jax.ShapeDtypeStruct((k // LANES, LANES), f32)],
        scratch_shapes=[pltpu.VMEM((k, d), f32), pltpu.SemaphoreType.DMA((k // out_step,))] + scratch(rows, k, d),
        compiler_params=pltpu.CompilerParams(vmem_limit_bytes=20 * 2**20),
        cost_estimate=cost(rows, k, d),
        name="last",
    )(*[in_vmem(a) for a in args])
    return numerator, weights.reshape(k)


def after(v, other):
    return lax.optimization_barrier((v, other))[0]


def body(rows, lognorm, centroids, counts):
    def send(v, how):
        return lax.ppermute(v, AXES, how)

    own = lax.all_to_all(pack(rows, lognorm, 16), AXES, 0, 0, axis_index_groups=FIRST, tiled=True)
    own = join(own)
    prepared = prepare(centroids, counts)
    up, down = send(own, FORWARD), send(own, BACKWARD)
    sums = chunk([own, send(own, SWAP)], *prepared, ())
    for _ in range(2):
        up, down, sums = after(up, sums), after(down, sums), after(sums, (up, down))
        blocks = [after(up, down), after(down, up)]
        up, down = send(up, FORWARD), send(down, BACKWARD)
        sums = chunk(blocks + [send(b, SWAP) for b in blocks], *prepared, sums)
    up, down, sums = after(up, sums), after(down, sums), after(sums, (up, down))
    far = send(down, BACKWARD)
    up, down = after(up, down), after(down, up)
    swapped = [send(up, SWAP), send(down, SWAP)]
    sums = chunk([up, down], *prepared, sums)
    sums = chunk(swapped, *prepared, sums)
    far, sums = after(far, sums), after(sums, far)
    return last([far, send(far, SWAP)], *prepared, sums)


def solution(mesh):
    split = Mesh(mesh.devices.reshape(4, 2, 8, 2, 2), AXES)
    blk = ("x", "yh", "z", "core")
    in_specs = (P(AXES, None), P(AXES), P(blk, None), P(blk))
    out_specs = (P(blk, None), P(blk))
    return jax.shard_map(body, mesh=split, in_specs=in_specs, out_specs=out_specs, check_vma=False)
```

```python
import functools

import jax
import jax.numpy as jnp
from jax import lax
from jax.experimental import pallas as pl
from jax.experimental.pallas import tpu as pltpu
from jax.sharding import Mesh, PartitionSpec as P

f32, bf16 = jnp.float32, jnp.bfloat16
AXES = ("x", "yh", "z", "core", "yl")
NT = (((1,), (1,)), ((), ()))
NN = (((1,), (0,)), ((), ()))
LANES = 128
VMEM = pl.BlockSpec(memory_space=pltpu.VMEM)


def flat(x, y, z, c):
    return ((x % 4 * 2 + y % 4 // 2) * 8 + z % 8) * 4 + c * 2 + y % 2


def pairs(target):
    return [
        (flat(x, y, z, c), flat(*target(x, y, z, c)))
        for x in range(4) for y in range(4) for z in range(8) for c in range(2)
    ]


LOOP = [(0, 0), (1, 0), (2, 0), (3, 0), (3, 1), (2, 1), (1, 1), (0, 1)]


def ring(step, along_z=0):
    def target(x, y, z, c):
        if c == along_z:
            return x, y, z + step, c
        yh, yl = y // 2, y % 2
        nx, nh = LOOP[(LOOP.index(((x + 2 * yl) % 4, yh)) + step) % 8]
        return nx + 2 * yl, nh * 2 + yl, z, c
    return pairs(target)


FORWARD, BACKWARD = ring(1), ring(-1)
OTHER_FORWARD = ring(1, along_z=1)
SWAP = pairs(lambda x, y, z, c: (x, y, z, 1 - c))
FIRST = [[flat(x, y, z, 0) for x in range(4) for y in range(4)] for z in range(8)] + [
    [flat(x, 2 * yh + yl, z, 1) for z in range(8) for yl in range(2)] for x in range(4) for yh in range(2)
]


def halves(v):
    high = v.astype(bf16)
    return high, (v - high.astype(f32)).astype(bf16)


def dot(a, b, dims):
    return lax.dot_general(a, b, dims, preferred_element_type=f32)


def product(a_high, a_low, b_high, b_low, dims):
    return dot(a_high, b_high, dims) + dot(a_low, b_high, dims) + dot(a_high, b_low, dims)


def prepare_kernel(parts, shard, counts, high, low, penalty, landed, sems):
    n = shard.shape[0] // parts
    places = [pl.ds(i * n, n) for i in range(parts)]
    copies = [pltpu.make_async_copy(shard.at[at, :], landed.at[at, :], sems.at[i]) for i, at in enumerate(places)]
    for copy in copies:
        copy.start()
    pen = 0.5 * jnp.log(1.0 + counts[...].astype(f32))
    for i in range(pen.shape[0]):
        penalty[pl.ds(i * LANES, LANES), :] = jnp.transpose(jnp.broadcast_to(pen[i : i + 1, :], (LANES, LANES)))
    for copy, at in zip(copies, places):
        copy.wait()
        high[at, :], low[at, :] = halves(landed[at, :])


def prepare(shard, counts):
    k, d = shard.shape
    parts = 8
    return pl.pallas_call(
        functools.partial(prepare_kernel, parts),
        in_specs=[pl.BlockSpec(memory_space=pl.ANY), VMEM],
        out_specs=[VMEM] * 3,
        out_shape=[pltpu.VMEM((k, d), bf16), pltpu.VMEM((k, d), bf16), pltpu.VMEM((k, LANES), f32)],
        scratch_shapes=[pltpu.VMEM((k, d), f32), pltpu.SemaphoreType.DMA((parts,))],
        compiler_params=pltpu.CompilerParams(vmem_limit_bytes=8 * 2**20),
        cost_estimate=pl.CostEstimate(flops=4 * k * d, bytes_accessed=8 * k * d, transcendentals=0),
        name="prepare",
    )(pltpu.with_memory_space_constraint(shard, pltpu.HBM), counts.reshape(k // LANES, LANES))


def pack_kernel(rows, norms, packed):
    n, d = rows.shape
    diagonal = lax.broadcasted_iota(jnp.int32, (n, n), 0) == lax.broadcasted_iota(jnp.int32, (n, n), 1)
    norm = jnp.sum(jnp.where(diagonal, norms[...], 0.0), axis=1, keepdims=True)
    packed[:, :, :d] = jnp.broadcast_to(rows[...][None], (packed.shape[0], n, d))
    packed[:, :, d:] = jnp.broadcast_to(norm[None], (packed.shape[0], n, LANES))


def pack(rows, lognorm, copies):
    n, d = rows.shape
    return pl.pallas_call(
        pack_kernel,
        in_specs=[VMEM] * 2,
        out_specs=VMEM,
        out_shape=pltpu.VMEM((copies, n, d + LANES), f32),
        name="pack",
    )(rows, lognorm.reshape(1, n))


MARGIN = 8


def join_kernel(parts, joined):
    count, n, width = parts.shape
    rows = count * n
    groups = width // LANES - 1
    for i in range(groups):
        joined[pl.ds(i * rows, rows), :] = parts[:, :, i * LANES : (i + 1) * LANES].reshape(rows, LANES)
    norms = parts[:, :, groups * LANES :].reshape(rows, LANES)
    joined[pl.ds(groups * rows, MARGIN), :] = jnp.transpose(norms)[:MARGIN, :]


def join(parts):
    count, n, width = parts.shape
    return pl.pallas_call(
        join_kernel,
        in_specs=[VMEM],
        out_specs=VMEM,
        out_shape=pltpu.VMEM((count * n * (width // LANES - 1) + MARGIN, LANES), f32),
        name="join",
    )(in_vmem(parts))


def in_vmem(v):
    return pltpu.with_memory_space_constraint(v, pltpu.VMEM)


def load_rows(blocks, row_high, row_low):
    norms = []
    for i, block in enumerate(blocks):
        size = block.shape[0] - MARGIN
        rows = jnp.concatenate([block[j : j + LANES, :] for j in range(0, size, LANES)], axis=1)
        at = pl.ds(i * LANES, LANES)
        row_high[at, :], row_low[at, :] = halves(rows)
        norms.append(block[size : size + 1, :])
    return jnp.concatenate(norms, axis=1)


def respond(high, low, penalty, norms, row_high, row_low, resp_high, resp_low, at):
    score = product(high[at, :], low[at, :], row_high[...], row_low[...], NT)
    resp = jnp.exp(score - penalty[at, 0:1] - norms)
    resp_high[at, :], resp_low[at, :] = halves(resp)
    return sum(resp[:, i : i + LANES] for i in range(0, resp.shape[1], LANES))


def gather_up(row_high, row_low, resp_high, resp_low, at):
    return product(resp_high[at, :], resp_low[at, :], row_high[...], row_low[...], NN)


def chunk_kernel(count, fresh, step, *refs):
    blocks, refs = refs[:count], refs[count:]
    if fresh:
        high, low, penalty, total_out, mass_out, *work = refs
    else:
        high, low, penalty, total_in, mass_in, total_out, mass_out, *work = refs
    norms = load_rows(blocks, *work[:2])
    places = [pl.ds(start, step) for start in range(0, high.shape[0], step)]
    for at in places:
        mass = respond(high, low, penalty, norms, *work, at)
        mass_out[at, :] = mass if fresh else mass_in[at, :] + mass
    for at in places:
        total = gather_up(*work, at)
        total_out[at, :] = total if fresh else total_in[at, :] + total


def scratch(rows, k, d):
    return [pltpu.VMEM((rows, d), bf16)] * 2 + [pltpu.VMEM((k, rows), bf16)] * 2


def cost(rows, k, d):
    return pl.CostEstimate(flops=12 * rows * k * d, bytes_accessed=4 * rows * d, transcendentals=rows * k)


def chunk(blocks, high, low, penalty, sums):
    k, d = high.shape
    count, rows = len(blocks), LANES * len(blocks)
    args = [*blocks, high, low, penalty, *sums]
    return pl.pallas_call(
        functools.partial(chunk_kernel, count, not sums, 512),
        in_specs=[VMEM] * len(args),
        out_specs=[VMEM] * 2,
        out_shape=[pltpu.VMEM((k, d), f32), pltpu.VMEM((k, LANES), f32)],
        scratch_shapes=scratch(rows, k, d),
        input_output_aliases={count + 3: 0, count + 4: 1} if sums else {},
        compiler_params=pltpu.CompilerParams(vmem_limit_bytes=20 * 2**20),
        cost_estimate=cost(rows, k, d),
        name="chunk",
    )(*[in_vmem(a) for a in args])


def last_kernel(count, step, out_step, *refs):
    blocks, refs = refs[:count], refs[count:]
    high, low, penalty, total_in, mass_in, total_out, mass_out, done, sems, *work = refs
    norms = load_rows(blocks, *work[:2])
    k = high.shape[0]
    for start in range(0, k, step):
        at = pl.ds(start, step)
        mass = mass_in[at, :] + respond(high, low, penalty, norms, *work, at)
        for j in range(step // LANES):
            part = jnp.transpose(mass[j * LANES : (j + 1) * LANES, :])
            mass_out[pl.ds(start // LANES + j, 1), :] = jnp.sum(part, axis=0, keepdims=True)
    copies = []
    for i, start in enumerate(range(0, k, out_step)):
        at = pl.ds(start, out_step)
        done[at, :] = total_in[at, :] + gather_up(*work, at)
        copies.append(pltpu.make_async_copy(done.at[at, :], total_out.at[at, :], sems.at[i]))
        copies[-1].start()
    for copy in copies:
        copy.wait()


def last(blocks, high, low, penalty, sums):
    k, d = high.shape
    step, out_step = 512, 128
    count, rows = len(blocks), LANES * len(blocks)
    args = [*blocks, high, low, penalty, *sums]
    numerator, weights = pl.pallas_call(
        functools.partial(last_kernel, count, step, out_step),
        in_specs=[VMEM] * len(args),
        out_specs=[pl.BlockSpec(memory_space=pl.ANY), VMEM],
        out_shape=[jax.ShapeDtypeStruct((k, d), f32), jax.ShapeDtypeStruct((k // LANES, LANES), f32)],
        scratch_shapes=[pltpu.VMEM((k, d), f32), pltpu.SemaphoreType.DMA((k // out_step,))] + scratch(rows, k, d),
        compiler_params=pltpu.CompilerParams(vmem_limit_bytes=20 * 2**20),
        cost_estimate=cost(rows, k, d),
        name="last",
    )(*[in_vmem(a) for a in args])
    return numerator, weights.reshape(k)


def after(v, other):
    return lax.optimization_barrier((v, other))[0]


def body(rows, lognorm, centroids, counts):
    def send(v, how):
        return lax.ppermute(v, AXES, how)

    own = lax.all_to_all(pack(rows, lognorm, 16), AXES, 0, 0, axis_index_groups=FIRST, tiled=True)
    own = join(own)
    prepared = prepare(centroids, counts)
    up, down = send(own, FORWARD), send(own, BACKWARD)
    sums = chunk([own, send(own, SWAP)], *prepared, ())
    for _ in range(2):
        up, down, sums = after(up, sums), after(down, sums), after(sums, (up, down))
        blocks = [up, down]
        up, down = send(up, FORWARD), send(down, BACKWARD)
        sums = chunk(blocks + [send(b, SWAP) for b in blocks], *prepared, sums)
    up, down, sums = after(up, sums), after(down, sums), after(sums, (up, down))
    far = send(down, BACKWARD)
    swapped = [send(up, SWAP), send(down, SWAP)]
    other_far = send(swapped[0], OTHER_FORWARD)
    sums = chunk([up, swapped[0]], *prepared, sums)
    sums = chunk([down, swapped[1]], *prepared, sums)
    far, other_far, sums = lax.optimization_barrier((far, other_far, sums))
    return last([far, other_far], *prepared, sums)


def solution(mesh):
    split = Mesh(mesh.devices.reshape(4, 2, 8, 2, 2), AXES)
    blk = ("x", "yh", "z", "core")
    in_specs = (P(AXES, None), P(AXES), P(blk, None), P(blk))
    out_specs = (P(blk, None), P(blk))
    return jax.shard_map(body, mesh=split, in_specs=in_specs, out_specs=out_specs, check_vma=False)
```

```python
import functools

import jax
import jax.numpy as jnp
from jax import lax
from jax.experimental import pallas as pl
from jax.experimental.pallas import tpu as pltpu
from jax.sharding import Mesh, PartitionSpec as P

f32, bf16 = jnp.float32, jnp.bfloat16
AXES = ("x", "yh", "z", "core", "yl")
NT = (((1,), (1,)), ((), ()))
NN = (((1,), (0,)), ((), ()))
LANES = 128
VMEM = pl.BlockSpec(memory_space=pltpu.VMEM)


def flat(x, y, z, c):
    return ((x % 4 * 2 + y % 4 // 2) * 8 + z % 8) * 4 + c * 2 + y % 2


def pairs(target):
    return [
        (flat(x, y, z, c), flat(*target(x, y, z, c)))
        for x in range(4) for y in range(4) for z in range(8) for c in range(2)
    ]


LOOP = [(0, 0), (1, 0), (2, 0), (3, 0), (3, 1), (2, 1), (1, 1), (0, 1)]


def ring(step, along_z=0):
    def target(x, y, z, c):
        if c == along_z:
            return x, y, z + step, c
        yh, yl = y // 2, y % 2
        nx, nh = LOOP[(LOOP.index(((x + 2 * yl) % 4, yh)) + step) % 8]
        return nx + 2 * yl, nh * 2 + yl, z, c
    return pairs(target)


FORWARD, BACKWARD = ring(1), ring(-1)
OTHER_FORWARD = ring(1, along_z=1)
SWAP = pairs(lambda x, y, z, c: (x, y, z, 1 - c))
FIRST = [[flat(x, y, z, 0) for x in range(4) for y in range(4)] for z in range(8)] + [
    [flat(x, 2 * yh + yl, z, 1) for z in range(8) for yl in range(2)] for x in range(4) for yh in range(2)
]


def halves(v):
    high = v.astype(bf16)
    return high, (v - high.astype(f32)).astype(bf16)


def dot(a, b, dims):
    return lax.dot_general(a, b, dims, preferred_element_type=f32)


def product(a_high, a_low, b_high, b_low, dims):
    return dot(a_high, b_high, dims) + dot(a_low, b_high, dims) + dot(a_high, b_low, dims)


def prepare_kernel(parts, shard, counts, high, low, penalty, landed, sizes, sems):
    first = pltpu.make_async_copy(counts, sizes, sems.at[parts])
    first.start()
    n = shard.shape[0] // parts
    places = [pl.ds(i * n, n) for i in range(parts)]
    copies = [pltpu.make_async_copy(shard.at[at, :], landed.at[at, :], sems.at[i]) for i, at in enumerate(places)]
    for copy in copies:
        copy.start()
    first.wait()
    pen = 0.5 * jnp.log(1.0 + sizes[...].astype(f32))
    for i in range(pen.shape[0]):
        penalty[pl.ds(i * LANES, LANES), :] = jnp.transpose(jnp.broadcast_to(pen[i : i + 1, :], (LANES, LANES)))
    for copy, at in zip(copies, places):
        copy.wait()
        high[at, :], low[at, :] = halves(landed[at, :])


def prepare(shard, counts):
    k, d = shard.shape
    parts = 8
    return pl.pallas_call(
        functools.partial(prepare_kernel, parts),
        in_specs=[pl.BlockSpec(memory_space=pl.ANY)] * 2,
        out_specs=[VMEM] * 3,
        out_shape=[pltpu.VMEM((k, d), bf16), pltpu.VMEM((k, d), bf16), pltpu.VMEM((k, LANES), f32)],
        scratch_shapes=[
            pltpu.VMEM((k, d), f32),
            pltpu.VMEM((k // LANES, LANES), jnp.int32),
            pltpu.SemaphoreType.DMA((parts + 1,)),
        ],
        compiler_params=pltpu.CompilerParams(vmem_limit_bytes=8 * 2**20),
        cost_estimate=pl.CostEstimate(flops=4 * k * d, bytes_accessed=8 * k * d, transcendentals=0),
        name="prepare",
    )(in_hbm(shard), in_hbm(counts.reshape(k // LANES, LANES)))


def in_hbm(v):
    return pltpu.with_memory_space_constraint(v, pltpu.HBM)


def pack_kernel(rows, norms, packed):
    n, d = rows.shape
    diagonal = lax.broadcasted_iota(jnp.int32, (n, n), 0) == lax.broadcasted_iota(jnp.int32, (n, n), 1)
    norm = jnp.sum(jnp.where(diagonal, norms[...], 0.0), axis=1, keepdims=True)
    packed[:, :, :d] = jnp.broadcast_to(rows[...][None], (packed.shape[0], n, d))
    packed[:, :, d:] = jnp.broadcast_to(norm[None], (packed.shape[0], n, LANES))


def pack(rows, lognorm, copies):
    n, d = rows.shape
    return pl.pallas_call(
        pack_kernel,
        in_specs=[VMEM] * 2,
        out_specs=VMEM,
        out_shape=pltpu.VMEM((copies, n, d + LANES), f32),
        name="pack",
    )(rows, lognorm.reshape(1, n))


MARGIN = 8


def join_kernel(parts, joined):
    count, n, width = parts.shape
    rows = count * n
    groups = width // LANES - 1
    for i in range(groups):
        joined[pl.ds(i * rows, rows), :] = parts[:, :, i * LANES : (i + 1) * LANES].reshape(rows, LANES)
    norms = parts[:, :, groups * LANES :].reshape(rows, LANES)
    joined[pl.ds(groups * rows, MARGIN), :] = jnp.transpose(norms)[:MARGIN, :]


def join(parts):
    count, n, width = parts.shape
    return pl.pallas_call(
        join_kernel,
        in_specs=[VMEM],
        out_specs=VMEM,
        out_shape=pltpu.VMEM((count * n * (width // LANES - 1) + MARGIN, LANES), f32),
        name="join",
    )(in_vmem(parts))


def in_vmem(v):
    return pltpu.with_memory_space_constraint(v, pltpu.VMEM)


def load_rows(blocks, row_high, row_low):
    norms = []
    for i, block in enumerate(blocks):
        size = block.shape[0] - MARGIN
        rows = jnp.concatenate([block[j : j + LANES, :] for j in range(0, size, LANES)], axis=1)
        at = pl.ds(i * LANES, LANES)
        row_high[at, :], row_low[at, :] = halves(rows)
        norms.append(block[size : size + 1, :])
    return jnp.concatenate(norms, axis=1)


def respond(high, low, penalty, norms, row_high, row_low, resp_high, resp_low, at):
    score = product(high[at, :], low[at, :], row_high[...], row_low[...], NT)
    resp = jnp.exp(score - penalty[at, 0:1] - norms)
    resp_high[at, :], resp_low[at, :] = halves(resp)
    return sum(resp[:, i : i + LANES] for i in range(0, resp.shape[1], LANES))


def gather_up(row_high, row_low, resp_high, resp_low, at):
    return product(resp_high[at, :], resp_low[at, :], row_high[...], row_low[...], NN)


def chunk_kernel(count, fresh, step, *refs):
    blocks, refs = refs[:count], refs[count:]
    if fresh:
        high, low, penalty, total_out, mass_out, *work = refs
    else:
        high, low, penalty, total_in, mass_in, total_out, mass_out, *work = refs
    norms = load_rows(blocks, *work[:2])
    places = [pl.ds(start, step) for start in range(0, high.shape[0], step)]
    for at in places:
        mass = respond(high, low, penalty, norms, *work, at)
        mass_out[at, :] = mass if fresh else mass_in[at, :] + mass
    for at in places:
        total = gather_up(*work, at)
        total_out[at, :] = total if fresh else total_in[at, :] + total


def scratch(rows, k, d):
    return [pltpu.VMEM((rows, d), bf16)] * 2 + [pltpu.VMEM((k, rows), bf16)] * 2


def cost(rows, k, d):
    return pl.CostEstimate(flops=12 * rows * k * d, bytes_accessed=4 * rows * d, transcendentals=rows * k)


def chunk(blocks, high, low, penalty, sums):
    k, d = high.shape
    count, rows = len(blocks), LANES * len(blocks)
    args = [*blocks, high, low, penalty, *sums]
    return pl.pallas_call(
        functools.partial(chunk_kernel, count, not sums, min(k, 256 * count)),
        in_specs=[VMEM] * len(args),
        out_specs=[VMEM] * 2,
        out_shape=[pltpu.VMEM((k, d), f32), pltpu.VMEM((k, LANES), f32)],
        scratch_shapes=scratch(rows, k, d),
        input_output_aliases={count + 3: 0, count + 4: 1} if sums else {},
        compiler_params=pltpu.CompilerParams(vmem_limit_bytes=20 * 2**20),
        cost_estimate=cost(rows, k, d),
        name="chunk",
    )(*[in_vmem(a) for a in args])


def last_kernel(count, step, out_step, *refs):
    blocks, refs = refs[:count], refs[count:]
    high, low, penalty, total_in, mass_in, total_out, mass_out, done, sems, *work = refs
    norms = load_rows(blocks, *work[:2])
    k = high.shape[0]
    for start in range(0, k, step):
        at = pl.ds(start, step)
        mass = mass_in[at, :] + respond(high, low, penalty, norms, *work, at)
        for j in range(step // LANES):
            part = jnp.transpose(mass[j * LANES : (j + 1) * LANES, :])
            mass_out[pl.ds(start // LANES + j, 1), :] = jnp.sum(part, axis=0, keepdims=True)
    copies = []
    for i, start in enumerate(range(0, k, out_step)):
        at = pl.ds(start, out_step)
        done[at, :] = total_in[at, :] + gather_up(*work, at)
        copies.append(pltpu.make_async_copy(done.at[at, :], total_out.at[at, :], sems.at[i]))
        copies[-1].start()
    for copy in copies:
        copy.wait()


def last(blocks, high, low, penalty, sums):
    k, d = high.shape
    step, out_step = 512, 128
    count, rows = len(blocks), LANES * len(blocks)
    args = [*blocks, high, low, penalty, *sums]
    numerator, weights = pl.pallas_call(
        functools.partial(last_kernel, count, step, out_step),
        in_specs=[VMEM] * len(args),
        out_specs=[pl.BlockSpec(memory_space=pl.ANY), VMEM],
        out_shape=[jax.ShapeDtypeStruct((k, d), f32), jax.ShapeDtypeStruct((k // LANES, LANES), f32)],
        scratch_shapes=[pltpu.VMEM((k, d), f32), pltpu.SemaphoreType.DMA((k // out_step,))] + scratch(rows, k, d),
        compiler_params=pltpu.CompilerParams(vmem_limit_bytes=20 * 2**20),
        cost_estimate=cost(rows, k, d),
        name="last",
    )(*[in_vmem(a) for a in args])
    return numerator, weights.reshape(k)


def after(v, other):
    return lax.optimization_barrier((v, other))[0]


def body(rows, lognorm, centroids, counts):
    def send(v, how):
        return lax.ppermute(v, AXES, how)

    own = lax.all_to_all(pack(rows, lognorm, 16), AXES, 0, 0, axis_index_groups=FIRST, tiled=True)
    own = join(own)
    prepared = prepare(centroids, counts)
    up, down = send(own, FORWARD), send(own, BACKWARD)
    sums = chunk([own, send(own, SWAP)], *prepared, ())
    for _ in range(2):
        up, down, sums = after(up, sums), after(down, sums), after(sums, (up, down))
        blocks = [up, down]
        up, down = send(up, FORWARD), send(down, BACKWARD)
        sums = chunk(blocks + [send(b, SWAP) for b in blocks], *prepared, sums)
    up, down, sums = after(up, sums), after(down, sums), after(sums, (up, down))
    far = send(down, BACKWARD)
    swapped = [send(up, SWAP), send(down, SWAP)]
    other_far = send(swapped[0], OTHER_FORWARD)
    sums = chunk([up, swapped[0]], *prepared, sums)
    sums = chunk([down, swapped[1]], *prepared, sums)
    far, other_far, sums = lax.optimization_barrier((far, other_far, sums))
    return last([far, other_far], *prepared, sums)


def solution(mesh):
    split = Mesh(mesh.devices.reshape(4, 2, 8, 2, 2), AXES)
    blk = ("x", "yh", "z", "core")
    in_specs = (P(AXES, None), P(AXES), P(blk, None), P(blk))
    out_specs = (P(blk, None), P(blk))
    return jax.shard_map(body, mesh=split, in_specs=in_specs, out_specs=out_specs, check_vma=False)
```

```python
import functools

import jax
import jax.numpy as jnp
from jax import lax
from jax.experimental import pallas as pl
from jax.experimental.pallas import tpu as pltpu
from jax.sharding import Mesh, PartitionSpec as P

f32, bf16 = jnp.float32, jnp.bfloat16
AXES = ("x", "yh", "z", "core", "yl")
NT = (((1,), (1,)), ((), ()))
NN = (((1,), (0,)), ((), ()))
LANES = 128
VMEM = pl.BlockSpec(memory_space=pltpu.VMEM)


def flat(x, y, z, c):
    return ((x % 4 * 2 + y % 4 // 2) * 8 + z % 8) * 4 + c * 2 + y % 2


def pairs(target):
    return [
        (flat(x, y, z, c), flat(*target(x, y, z, c)))
        for x in range(4) for y in range(4) for z in range(8) for c in range(2)
    ]


LOOP = [(0, 0), (1, 0), (2, 0), (3, 0), (3, 1), (2, 1), (1, 1), (0, 1)]


def ring(step, along_z=0):
    def target(x, y, z, c):
        if c == along_z:
            return x, y, z + step, c
        yh, yl = y // 2, y % 2
        nx, nh = LOOP[(LOOP.index(((x + 2 * yl) % 4, yh)) + step) % 8]
        return nx + 2 * yl, nh * 2 + yl, z, c
    return pairs(target)


FORWARD, BACKWARD = ring(1), ring(-1)
OTHER_FORWARD = ring(1, along_z=1)
SWAP = pairs(lambda x, y, z, c: (x, y, z, 1 - c))
FIRST = [[flat(x, y, z, 0) for x in range(4) for y in range(4)] for z in range(8)] + [
    [flat(x, 2 * yh + yl, z, 1) for z in range(8) for yl in range(2)] for x in range(4) for yh in range(2)
]


def halves(v):
    high = v.astype(bf16)
    return high, (v - high.astype(f32)).astype(bf16)


def dot(a, b, dims):
    return lax.dot_general(a, b, dims, preferred_element_type=f32)


def product(a_high, a_low, b_high, b_low, dims):
    return dot(a_high, b_high, dims) + dot(a_low, b_high, dims) + dot(a_high, b_low, dims)


def prepare_kernel(parts, shard, counts, high, low, penalty, landed, sizes, sems):
    first = pltpu.make_async_copy(counts, sizes, sems.at[parts])
    first.start()
    n = shard.shape[0] // parts
    places = [pl.ds(i * n, n) for i in range(parts)]
    copies = [pltpu.make_async_copy(shard.at[at, :], landed.at[at, :], sems.at[i]) for i, at in enumerate(places)]
    for copy in copies:
        copy.start()
    first.wait()
    pen = 0.5 * jnp.log(1.0 + sizes[...].astype(f32))
    for i in range(pen.shape[0]):
        penalty[pl.ds(i * LANES, LANES), :] = jnp.transpose(jnp.broadcast_to(pen[i : i + 1, :], (LANES, LANES)))
    for copy, at in zip(copies, places):
        copy.wait()
        high[at, :], low[at, :] = halves(landed[at, :])


def prepare(shard, counts):
    k, d = shard.shape
    parts = 8
    return pl.pallas_call(
        functools.partial(prepare_kernel, parts),
        in_specs=[pl.BlockSpec(memory_space=pl.ANY)] * 2,
        out_specs=[VMEM] * 3,
        out_shape=[pltpu.VMEM((k, d), bf16), pltpu.VMEM((k, d), bf16), pltpu.VMEM((k, LANES), f32)],
        scratch_shapes=[
            pltpu.VMEM((k, d), f32),
            pltpu.VMEM((k // LANES, LANES), jnp.int32),
            pltpu.SemaphoreType.DMA((parts + 1,)),
        ],
        compiler_params=pltpu.CompilerParams(vmem_limit_bytes=8 * 2**20),
        cost_estimate=pl.CostEstimate(flops=4 * k * d, bytes_accessed=8 * k * d, transcendentals=0),
        name="prepare",
    )(in_hbm(shard), in_hbm(counts.reshape(k // LANES, LANES)))


def in_hbm(v):
    return pltpu.with_memory_space_constraint(v, pltpu.HBM)


def pack_kernel(rows, norms, packed):
    n, d = rows.shape
    diagonal = lax.broadcasted_iota(jnp.int32, (n, n), 0) == lax.broadcasted_iota(jnp.int32, (n, n), 1)
    norm = jnp.sum(jnp.where(diagonal, norms[...], 0.0), axis=1, keepdims=True)
    packed[:, :, :d] = jnp.broadcast_to(rows[...][None], (packed.shape[0], n, d))
    packed[:, :, d:] = jnp.broadcast_to(norm[None], (packed.shape[0], n, LANES))


def pack(rows, lognorm, copies):
    n, d = rows.shape
    return pl.pallas_call(
        pack_kernel,
        in_specs=[VMEM] * 2,
        out_specs=VMEM,
        out_shape=pltpu.VMEM((copies, n, d + LANES), f32),
        name="pack",
    )(rows, lognorm.reshape(1, n))


MARGIN = 8


def join_kernel(parts, joined):
    count, n, width = parts.shape
    rows = count * n
    groups = width // LANES - 1
    for i in range(groups):
        joined[pl.ds(i * rows, rows), :] = parts[:, :, i * LANES : (i + 1) * LANES].reshape(rows, LANES)
    norms = parts[:, :, groups * LANES :].reshape(rows, LANES)
    joined[pl.ds(groups * rows, MARGIN), :] = jnp.transpose(norms)[:MARGIN, :]


def join(parts):
    count, n, width = parts.shape
    return pl.pallas_call(
        join_kernel,
        in_specs=[VMEM],
        out_specs=VMEM,
        out_shape=pltpu.VMEM((count * n * (width // LANES - 1) + MARGIN, LANES), f32),
        name="join",
    )(in_vmem(parts))


def in_vmem(v):
    return pltpu.with_memory_space_constraint(v, pltpu.VMEM)


def load_rows(blocks, row_high, row_low):
    norms = []
    for i, block in enumerate(blocks):
        size = block.shape[0] - MARGIN
        rows = jnp.concatenate([block[j : j + LANES, :] for j in range(0, size, LANES)], axis=1)
        at = pl.ds(i * LANES, LANES)
        row_high[at, :], row_low[at, :] = halves(rows)
        norms.append(block[size : size + 1, :])
    return jnp.concatenate(norms, axis=1)


def respond(high, low, penalty, norms, row_high, row_low, resp_high, resp_low, at):
    score = product(high[at, :], low[at, :], row_high[...], row_low[...], NT)
    resp = jnp.exp(score - penalty[at, 0:1] - norms)
    resp_high[at, :], resp_low[at, :] = halves(resp)
    return sum(resp[:, i : i + LANES] for i in range(0, resp.shape[1], LANES))


def gather_up(row_high, row_low, resp_high, resp_low, at):
    return product(resp_high[at, :], resp_low[at, :], row_high[...], row_low[...], NN)


def chunk_kernel(count, fresh, step, *refs):
    blocks, refs = refs[:count], refs[count:]
    if fresh:
        high, low, penalty, total_out, mass_out, *work = refs
    else:
        high, low, penalty, total_in, mass_in, total_out, mass_out, *work = refs
    norms = load_rows(blocks, *work[:2])
    places = [pl.ds(start, step) for start in range(0, high.shape[0], step)]
    for at in places:
        mass = respond(high, low, penalty, norms, *work, at)
        mass_out[at, :] = mass if fresh else mass_in[at, :] + mass
    for at in places:
        total = gather_up(*work, at)
        total_out[at, :] = total if fresh else total_in[at, :] + total


def scratch(rows, k, d):
    return [pltpu.VMEM((rows, d), bf16)] * 2 + [pltpu.VMEM((k, rows), bf16)] * 2


def cost(rows, k, d):
    return pl.CostEstimate(flops=rows * k, bytes_accessed=rows, transcendentals=0)


def chunk(blocks, high, low, penalty, sums):
    k, d = high.shape
    count, rows = len(blocks), LANES * len(blocks)
    args = [*blocks, high, low, penalty, *sums]
    return pl.pallas_call(
        functools.partial(chunk_kernel, count, not sums, min(k, 256 * count)),
        in_specs=[VMEM] * len(args),
        out_specs=[VMEM] * 2,
        out_shape=[pltpu.VMEM((k, d), f32), pltpu.VMEM((k, LANES), f32)],
        scratch_shapes=scratch(rows, k, d),
        input_output_aliases={count + 3: 0, count + 4: 1} if sums else {},
        compiler_params=pltpu.CompilerParams(vmem_limit_bytes=20 * 2**20),
        cost_estimate=cost(rows, k, d),
        name="chunk",
    )(*[in_vmem(a) for a in args])


def last_kernel(count, step, out_step, *refs):
    blocks, refs = refs[:count], refs[count:]
    high, low, penalty, total_in, mass_in, total_out, mass_out, done, sems, *work = refs
    norms = load_rows(blocks, *work[:2])
    k = high.shape[0]
    for start in range(0, k, step):
        at = pl.ds(start, step)
        mass = mass_in[at, :] + respond(high, low, penalty, norms, *work, at)
        for j in range(step // LANES):
            part = jnp.transpose(mass[j * LANES : (j + 1) * LANES, :])
            mass_out[pl.ds(start // LANES + j, 1), :] = jnp.sum(part, axis=0, keepdims=True)
    copies = []
    for i, start in enumerate(range(0, k, out_step)):
        at = pl.ds(start, out_step)
        done[at, :] = total_in[at, :] + gather_up(*work, at)
        copies.append(pltpu.make_async_copy(done.at[at, :], total_out.at[at, :], sems.at[i]))
        copies[-1].start()
    for copy in copies:
        copy.wait()


def last(blocks, high, low, penalty, sums):
    k, d = high.shape
    step, out_step = 512, 128
    count, rows = len(blocks), LANES * len(blocks)
    args = [*blocks, high, low, penalty, *sums]
    numerator, weights = pl.pallas_call(
        functools.partial(last_kernel, count, step, out_step),
        in_specs=[VMEM] * len(args),
        out_specs=[pl.BlockSpec(memory_space=pl.ANY), VMEM],
        out_shape=[jax.ShapeDtypeStruct((k, d), f32), jax.ShapeDtypeStruct((k // LANES, LANES), f32)],
        scratch_shapes=[pltpu.VMEM((k, d), f32), pltpu.SemaphoreType.DMA((k // out_step,))] + scratch(rows, k, d),
        compiler_params=pltpu.CompilerParams(vmem_limit_bytes=20 * 2**20),
        cost_estimate=cost(rows, k, d),
        name="last",
    )(*[in_vmem(a) for a in args])
    return numerator, weights.reshape(k)


def after(v, other):
    return lax.optimization_barrier((v, other))[0]


def body(rows, lognorm, centroids, counts):
    def send(v, how):
        return lax.ppermute(v, AXES, how)

    own = lax.all_to_all(pack(rows, lognorm, 16), AXES, 0, 0, axis_index_groups=FIRST, tiled=True)
    own = join(own)
    prepared = prepare(centroids, counts)
    up, down = send(own, FORWARD), send(own, BACKWARD)
    sums = chunk([own, send(own, SWAP)], *prepared, ())
    for _ in range(2):
        up, down, sums = after(up, sums), after(down, sums), after(sums, (up, down))
        blocks = [up, down]
        up, down = send(up, FORWARD), send(down, BACKWARD)
        sums = chunk(blocks + [send(b, SWAP) for b in blocks], *prepared, sums)
    up, down, sums = after(up, sums), after(down, sums), after(sums, (up, down))
    far = send(down, BACKWARD)
    swapped = [send(up, SWAP), send(down, SWAP)]
    other_far = send(swapped[0], OTHER_FORWARD)
    sums = chunk([up, swapped[0]], *prepared, sums)
    sums = chunk([down, swapped[1]], *prepared, sums)
    far, other_far, sums = lax.optimization_barrier((far, other_far, sums))
    return last([far, other_far], *prepared, sums)


def solution(mesh):
    split = Mesh(mesh.devices.reshape(4, 2, 8, 2, 2), AXES)
    blk = ("x", "yh", "z", "core")
    in_specs = (P(AXES, None), P(AXES), P(blk, None), P(blk))
    out_specs = (P(blk, None), P(blk))
    return jax.shard_map(body, mesh=split, in_specs=in_specs, out_specs=out_specs, check_vma=False)
```
